32 devices in a mesh: seq: 8 (over y, x, core), ch: 4 (over z).
Axes of the slice: x: 2, y: 2, z: 4, core: 2. Of those that a mesh axis runs over, the one named last changes fastest.
Arguments:
- token_ids: int32 [8192], P('seq'), may hold values from 0 to 511
- embedding: bfloat16 [4096, 512], P('ch'), may hold values from -26 to 26
- projected: bfloat16 [3, 4096, 512], P(None, 'ch'), may hold values from -6 to 6
- short_taps: float32 [7, 3, 4096], P(None, None, 'ch'), may hold values from -2 to 2
- long_filter: bfloat16 [4096, 8192], P('ch', 'seq'), may hold values from -1.6 to 1.6
- skip_gain: float32 [4096], P('ch'), may hold values from -3 to 3
Outputs:
- mixed: bfloat16 [4096, 8192], P('ch', 'seq')
The draws below stay inside these ranges and needn't reach their ends.
All inputs are finite; a program needn't handle non-finite values.
Results may differ from the reference program's by a relative error of at most 0.0075.
Values may be sent and summed in bfloat16 or wider, within the bound.
A program may use at most 192 MiB of HBM per device.

```python
import math
import jax
import jax.numpy as jnp
import numpy as np
from jax import lax

MIXER_CHANNELS = 4096
VOCAB = 512
TAPS = 7
TOKENS = 8192


def draw_embedding(key, part):
    stochastic_seeds = jax.random.split(key, 3)
    channel_pos = jnp.arange(MIXER_CHANNELS, dtype=jnp.float32)
    rising = 1.0 + 2.0 * channel_pos / (MIXER_CHANNELS - 1)
    channel_scale = jnp.exp(jax.random.uniform(stochastic_seeds[0], (MIXER_CHANNELS, 1), minval=0.0, maxval=math.log(10.0)))
    vocab_factor = jnp.exp(jax.random.uniform(stochastic_seeds[1], (1, VOCAB), minval=math.log(0.7), maxval=math.log(1.4)))
    rough_part = jnp.clip(jax.random.normal(stochastic_seeds[2], (MIXER_CHANNELS, VOCAB)), -6.0, 6.0)
    return (rough_part * channel_scale * rising[:, None] * vocab_factor * 0.1).astype(jnp.bfloat16)


def draw_long_filter(key, part):
    stochastic_seeds = jax.random.split(key, 4)
    filter_extent = TOKENS
    log_rate = jax.random.uniform(stochastic_seeds[0], (MIXER_CHANNELS, 1), minval=math.log(0.1 / filter_extent), maxval=math.log(1.0 / 30.0))
    rough_part = jnp.clip(jax.random.normal(stochastic_seeds[3], (MIXER_CHANNELS, filter_extent)), -6.0, 6.0)
    fading_speed = jnp.exp(log_rate)
    spike_offsets = jnp.arange(filter_extent, dtype=jnp.float32)[None, :]
    fading_profile = -fading_speed * spike_offsets
    spike_onsets = jax.random.randint(stochastic_seeds[1], (MIXER_CHANNELS, 3), 1, filter_extent)
    spike_attenuations = jnp.log(jax.random.uniform(stochastic_seeds[2], (MIXER_CHANNELS, 3), minval=0.5, maxval=0.8))
    for spike_counter in range(3):
        fading_profile = fading_profile + jnp.where(spike_offsets >= spike_onsets[:, spike_counter:spike_counter + 1].astype(jnp.float32), spike_attenuations[:, spike_counter:spike_counter + 1], 0.0)
    normalizer = jnp.sqrt((1.0 - jnp.exp(-2.0 * fading_speed)) / (1.0 - jnp.exp(-2.0 * fading_speed * filter_extent)))
    return (normalizer * jnp.exp(fading_profile) * rough_part).astype(jnp.bfloat16)


def touch_ends(drawn, rng, smallest, top_value):
    dims = drawn.shape
    spot = [jax.random.randint(jax.random.fold_in(rng, axis), (), 0, dims[axis]) for axis in range(len(dims))]
    drawn = drawn.at[tuple(spot)].set(smallest)
    longest = dims.index(max(dims))
    spot[longest] = (spot[longest] + 1) % dims[longest]
    return drawn.at[tuple(spot)].set(top_value)


def block_scale(own_key, dims, pieces, low, top_value):
    def one(dim, blocks):
        heights = jax.random.uniform(jax.random.fold_in(jax.random.fold_in(own_key, 6), dim), (blocks,), jnp.float32, low / len(pieces), top_value / len(pieces))
        return jnp.repeat(jnp.exp(heights), dims[dim] // blocks).reshape((-1,) + (1,) * (len(dims) - dim - 1))

    level = one(*pieces[0])
    for cut in pieces[1:]:
        level = level * one(*cut)
    return level


def rank_bounds(amount, lean):
    weights = [(1 << 20) // math.isqrt(standing ** lean) + 1 for standing in range(1, amount + 1)]
    deviation = 1 + sum(weights) // (1 << 30)
    return np.cumsum(np.array([max(1, weight // deviation) for weight in weights]))


def skewed_ids(rng, extent, amount, slope):
    listing = rank_bounds(amount, slope)
    pick = jax.random.randint(jax.random.fold_in(rng, 1), extent, 0, int(listing[amount - 1]))
    standing = jnp.searchsorted(jnp.asarray(listing, jnp.int32), pick, side="right")
    return jax.random.permutation(jax.random.fold_in(rng, 2), amount)[standing].astype(jnp.int32)


def noise(stream_key, dims, width, bound, cuts=(), kind=jnp.bfloat16):
    gain = block_scale(stream_key, dims, cuts, -0.22, 0.18) if cuts else 1.0
    drawn = jax.random.normal(stream_key, dims, jnp.float32) * width * gain
    return jnp.minimum(jnp.maximum(drawn, -bound), bound).astype(kind)


def setup_inputs(seed: int = 0) -> dict:
    arg_keys = jax.random.split(jax.random.key(seed), 7)
    return {
        "token_ids": touch_ends(skewed_ids(arg_keys[0], (TOKENS,), VOCAB, 2), jax.random.fold_in(arg_keys[0], 3), 0, VOCAB - 1).astype(jnp.int32),
        "embedding": draw_embedding(jax.random.fold_in(arg_keys[6], 71), 0),
        "projected": noise(arg_keys[2], (3, MIXER_CHANNELS, VOCAB), 1.0, 6.0, ((1, 4),)),
        "short_taps": noise(arg_keys[3], (TAPS, 3, MIXER_CHANNELS), TAPS ** -0.5, 2.0, ((2, 4),), jnp.float32),
        "long_filter": draw_long_filter(jax.random.fold_in(arg_keys[6], 71), 0),
        "skip_gain": noise(arg_keys[5], (MIXER_CHANNELS,), 0.5, 3.0, ((0, 4),), jnp.float32),
    }


EPSILON = 1e-06

def short_conv(padded, weights):
    tap_count = weights.shape[0]
    filter_extent = padded.shape[2] - (tap_count - 1)
    acc_sum = jnp.zeros(padded.shape[:2] + (filter_extent,), jnp.float32)
    for offset in range(tap_count):
        begin = tap_count - 1 - offset
        acc_sum = acc_sum + weights[offset][:, :, None] * padded[:, :, begin:begin + filter_extent].astype(jnp.float32)
    return acc_sum

def reference(token_ids, embedding, projected, short_taps, long_filter, skip_gain):
    values = embedding.astype(jnp.float32)
    vocab_scale = 1.0 / jnp.sqrt(lax.optimization_barrier(jnp.sum(values * values, axis=0)) / MIXER_CHANNELS + EPSILON)
    token_scale = vocab_scale[token_ids]
    block_size = math.gcd(MIXER_CHANNELS, 256)
    filter_extent = token_ids.shape[0]

    def one_block(block_index):
        channel_start = block_index * block_size
        row_slice = lax.dynamic_slice_in_dim(projected, channel_start, block_size, axis=1)
        features = (row_slice[:, :, token_ids].astype(jnp.float32) * token_scale).astype(jnp.bfloat16)
        padded = jnp.pad(features, ((0, 0), (0, 0), (TAPS - 1, 0)))
        weights = lax.dynamic_slice_in_dim(short_taps, channel_start, block_size, axis=2)
        conv_out = short_conv(padded, weights)
        gated_rows = (conv_out[1] * conv_out[2]).astype(jnp.bfloat16)
        filter_rows = lax.dynamic_slice_in_dim(long_filter, channel_start, block_size, axis=0).astype(jnp.float32)
        spectrum = jnp.fft.rfft(gated_rows.astype(jnp.float32), n=2 * filter_extent, axis=1) * jnp.fft.rfft(filter_rows, n=2 * filter_extent, axis=1)
        convolved = jnp.fft.irfft(spectrum, n=2 * filter_extent, axis=1)[:, :filter_extent]
        skip_rows = lax.dynamic_slice_in_dim(skip_gain, channel_start, block_size)
        long_out = (convolved + skip_rows[:, None] * gated_rows.astype(jnp.float32)).astype(jnp.bfloat16)
        return (conv_out[0] * long_out.astype(jnp.float32)).astype(jnp.bfloat16)
    result = lax.map(one_block, jnp.arange(MIXER_CHANNELS // block_size, dtype=jnp.int32))
    return result.reshape(MIXER_CHANNELS, filter_extent)
```

```python
import functools
import math

import jax
import jax.numpy as jnp
import numpy as np
from jax import lax
from jax.experimental import pallas as pl
from jax.experimental.pallas import tpu as pltpu
from jax.sharding import PartitionSpec as P

MIXER_CHANNELS = 4096
EPSILON = 1e-06
LANES = 128
GROUP = 16
BATCH = 4
VMEM_LIMIT = 56 * 1024 * 1024


def transform_tables(length):
    coarse = length // LANES
    k1 = np.arange(coarse)[:, None] + 0.25
    phi = 2.0 * np.pi * k1 * np.arange(coarse)[None, :] / coarse
    first = np.concatenate([np.cos(phi), -np.sin(phi)], axis=0)
    psi = 2.0 * np.pi * k1 * np.arange(LANES)[None, :] / length
    fine = np.arange(LANES)
    chi = 2.0 * np.pi * (fine[:, None] * fine[None, :] % LANES) / LANES
    c, s = np.cos(chi), np.sin(chi)
    second = np.block([[c, -s], [s, c]])
    second_inv = np.block([[c, s], [-s, c]])
    bf = jnp.bfloat16
    return (
        jnp.asarray(first, bf),
        jnp.asarray(first.T / length, bf),
        jnp.asarray(np.cos(psi), jnp.float32),
        jnp.asarray(np.sin(psi), jnp.float32),
        jnp.asarray(second, bf),
        jnp.asarray(second_inv, bf),
    )


def feature_kernel(group, taps, ids_ref, table_ref, taps_ref, first_ref, gated_ref, feats, carry):
    tokens = ids_ref.shape[-1]
    vocab = table_ref.shape[1]

    @pl.when(pl.program_id(0) == 0)
    def _():
        carry[...] = jnp.zeros_like(carry)

    ids = ids_ref[0]
    onehot = (lax.broadcasted_iota(jnp.int32, (vocab, tokens), 0) == ids).astype(jnp.bfloat16)
    feats[:, :LANES] = carry[...]
    feats[:, LANES:] = jnp.dot(table_ref[...], onehot, preferred_element_type=jnp.float32)
    carry[...] = feats[:, tokens:]
    rows = 8

    def stream(j, r):
        ext = feats[pl.ds(j * group + r, rows), :]
        weights = taps_ref[pl.ds(j * group + r, rows), :]
        acc = weights[:, 0:1] * ext[:, LANES:]
        for k in range(1, taps):
            acc = acc + weights[:, k : k + 1] * pltpu.roll(ext, k, 1)[:, LANES:]
        return acc

    @pl.loop(0, group // 16)
    def _(step):
        parts = []
        for half in range(2):
            r = pl.multiple_of(step * 16 + half * 8, 8)
            first_ref[0, pl.ds(r, rows), :] = stream(0, r)
            parts.append(stream(1, r) * stream(2, r))
        at = pl.multiple_of(step * 16, 16)
        gated_ref[0, pl.ds(at, 16), :] = jnp.concatenate(parts, axis=0).astype(jnp.bfloat16)


def conv_kernel(
    gated_ref, filter_ref, conv0_ref, skip_ref, t1_ref, t1i_ref, c_ref, s_ref, w2_ref, w2i_ref,
    out_ref, zs, hs, ys,
):
    blocks, group, tokens = gated_ref.shape
    per = tokens // LANES
    coarse = blocks * per
    f32, bf = jnp.float32, jnp.bfloat16

    for s in range(blocks):
        for q in range(per):
            cols = slice(q * LANES, (q + 1) * LANES)
            dst = pl.ds(s * per + q, group, stride=coarse)
            zs[dst, :] = gated_ref[s, :, cols].astype(f32)
            hs[dst, :] = filter_ref[s, :, cols].astype(f32)

    cos, sin = c_ref[...], s_ref[...]

    @pl.loop(0, group // BATCH)
    def _(step):
        base = pl.multiple_of(step * (BATCH * coarse), BATCH * coarse)
        parts = []
        for i in range(BATCH):
            at = pl.ds(base + i * coarse, coarse)
            both = jnp.concatenate([zs[at, :], hs[at, :]], axis=1).astype(bf)
            spread = jnp.dot(t1_ref[...], both, preferred_element_type=f32)
            for side in range(2):
                cols = slice(side * LANES, (side + 1) * LANES)
                re, im = spread[:coarse, cols], spread[coarse:, cols]
                parts.append(
                    jnp.concatenate([re * cos + im * sin, im * cos - re * sin], axis=1).astype(bf)
                )
        spectra = jnp.dot(jnp.concatenate(parts, axis=0), w2_ref[...], preferred_element_type=f32)
        parts = []
        for i in range(BATCH):
            z = spectra[2 * i * coarse : (2 * i + 1) * coarse]
            h = spectra[(2 * i + 1) * coarse : (2 * i + 2) * coarse]
            zr, zi, hr, hi = z[:, :LANES], z[:, LANES:], h[:, :LANES], h[:, LANES:]
            parts.append(jnp.concatenate([zr * hr - zi * hi, zr * hi + zi * hr], axis=1).astype(bf))
        back = jnp.dot(jnp.concatenate(parts, axis=0), w2i_ref[...], preferred_element_type=f32)
        for i in range(0, BATCH, 2):
            cols = []
            for o in range(2):
                p = back[(i + o) * coarse : (i + o + 1) * coarse]
                re, im = p[:, :LANES], p[:, LANES:]
                cols.append(jnp.concatenate([re * cos - im * sin, im * cos + re * sin], axis=0))
            res = jnp.dot(
                t1i_ref[...], jnp.concatenate(cols, axis=1).astype(bf), preferred_element_type=f32
            )
            for o in range(2):
                ys[pl.ds(base + (i + o) * coarse, coarse), :] = res[:, o * LANES : (o + 1) * LANES]

    skip = skip_ref[...]
    for s in range(blocks):
        for q in range(per):
            cols = slice(q * LANES, (q + 1) * LANES)
            conv = ys[pl.ds(s * per + q, group, stride=coarse), :]
            long_out = (conv + skip * gated_ref[s, :, cols].astype(f32)).astype(bf)
            out_ref[s, :, cols] = (conv0_ref[s, :, cols] * long_out.astype(f32)).astype(bf)


def features(ids, table, taps_rows, group, taps):
    blocks, _, tokens = ids.shape
    vocab = table.shape[1]
    return pl.pallas_call(
        functools.partial(feature_kernel, group, taps),
        grid=(blocks,),
        out_shape=(
            jax.ShapeDtypeStruct((blocks, group, tokens), jnp.float32),
            jax.ShapeDtypeStruct((blocks, group, tokens), jnp.bfloat16),
        ),
        in_specs=[
            pl.BlockSpec((1, 1, tokens), lambda i: (i, 0, 0)),
            pl.BlockSpec((3 * group, vocab), lambda i: (0, 0)),
            pl.BlockSpec((3 * group, taps), lambda i: (0, 0)),
        ],
        out_specs=(
            pl.BlockSpec((1, group, tokens), lambda i: (i, 0, 0)),
            pl.BlockSpec((1, group, tokens), lambda i: (i, 0, 0)),
        ),
        scratch_shapes=[
            pltpu.VMEM((3 * group, LANES + tokens), jnp.float32),
            pltpu.VMEM((3 * group, LANES), jnp.float32),
        ],
        compiler_params=pltpu.CompilerParams(vmem_limit_bytes=VMEM_LIMIT),
        cost_estimate=pl.CostEstimate(
            flops=2 * 3 * group * vocab * blocks * tokens,
            bytes_accessed=blocks * group * tokens * 6,
            transcendentals=0,
        ),
    )(ids, table, taps_rows)


def convolve(gated, filt, conv0, skip_rows):
    blocks, group, tokens = gated.shape
    length = blocks * tokens
    coarse = length // LANES
    tables = transform_tables(length)
    whole = lambda t: pl.BlockSpec(t.shape, lambda i: (0, 0))
    rows = pl.BlockSpec((blocks, GROUP, tokens), lambda i: (0, i, 0))
    return pl.pallas_call(
        conv_kernel,
        grid=(group // GROUP,),
        out_shape=jax.ShapeDtypeStruct((blocks, group, tokens), jnp.bfloat16),
        in_specs=[rows, rows, rows, pl.BlockSpec((GROUP, 1), lambda i: (i, 0))]
        + [whole(t) for t in tables],
        out_specs=rows,
        scratch_shapes=[pltpu.VMEM((GROUP * coarse, LANES), jnp.float32)] * 3,
        compiler_params=pltpu.CompilerParams(vmem_limit_bytes=VMEM_LIMIT),
        cost_estimate=pl.CostEstimate(
            flops=2 * group * coarse * 4 * 256 * 256,
            bytes_accessed=blocks * group * tokens * 10,
            transcendentals=0,
        ),
    )(gated, filt, conv0, skip_rows, *tables)


def shards(token_ids, embedding, projected, short_taps, long_filter, skip_gain):
    seq_count = lax.axis_size("seq")
    seq_index = lax.axis_index("seq")
    local_ch, vocab = embedding.shape
    tokens = token_ids.shape[0]
    taps = short_taps.shape[0]
    group = local_ch // seq_count
    start = seq_index * group

    filt = lax.all_to_all(
        long_filter.reshape(seq_count, group, tokens), "seq", split_axis=0, concat_axis=0, tiled=True
    )
    ids = lax.all_gather(token_ids.reshape(1, 1, tokens), "seq", axis=0, tiled=True)
    values = embedding.astype(jnp.float32)
    squares = lax.psum(jnp.sum(values * values, axis=0), "ch")
    vocab_scale = 1.0 / jnp.sqrt(squares / MIXER_CHANNELS + EPSILON)
    own = lax.dynamic_slice_in_dim(projected, start, group, axis=1)
    table = (own.astype(jnp.float32) * vocab_scale).astype(jnp.bfloat16)
    taps_rows = lax.dynamic_slice_in_dim(short_taps, start, group, axis=2).reshape(taps, 3 * group).T
    conv0, gated = features(ids, table.reshape(3 * group, vocab), taps_rows, group, taps)
    skip_rows = lax.dynamic_slice_in_dim(skip_gain, start, group)[:, None]
    mixed = convolve(gated, filt, conv0, skip_rows)
    returned = lax.all_to_all(mixed, "seq", split_axis=0, concat_axis=0, tiled=True)
    return returned.reshape(local_ch, tokens)


def solution(mesh):
    placed = (
        P("seq"),
        P("ch", None),
        P(None, "ch", None),
        P(None, None, "ch"),
        P("ch", "seq"),
        P("ch"),
    )
    return jax.shard_map(
        shards, mesh=mesh, in_specs=placed, out_specs=P("ch", "seq"), check_vma=False
    )
```

```python
import functools
import math

import jax
import jax.numpy as jnp
import numpy as np
from jax import lax
from jax.experimental import pallas as pl
from jax.experimental.pallas import tpu as pltpu
from jax.sharding import PartitionSpec as P

MIXER_CHANNELS = 4096
EPSILON = 1e-06
LANES = 128
GROUP = 16
BATCH = 4
HISTORY = 8
VMEM_LIMIT = 56 * 1024 * 1024
MESH = pl.DeviceIdType.MESH


def transform_tables(length):
    coarse = length // LANES
    k1 = np.arange(coarse)[:, None] + 0.25
    phi = 2.0 * np.pi * k1 * np.arange(coarse)[None, :] / coarse
    first = np.concatenate([np.cos(phi), -np.sin(phi)], axis=0)
    psi = 2.0 * np.pi * k1 * np.arange(LANES)[None, :] / length
    fine = np.arange(LANES)
    chi = 2.0 * np.pi * (fine[:, None] * fine[None, :] % LANES) / LANES
    c, s = np.cos(chi), np.sin(chi)
    second = np.block([[c, -s], [s, c]])
    second_inv = np.block([[c, s], [-s, c]])
    bf = jnp.bfloat16
    return (
        jnp.asarray(first, bf),
        jnp.asarray(first.T / length, bf),
        jnp.asarray(np.cos(psi), jnp.float32),
        jnp.asarray(np.sin(psi), jnp.float32),
        jnp.asarray(second, bf),
        jnp.asarray(second_inv, bf),
    )


def exchange_kernel(
    seq_count, ch_count, ids_ref, squares_ref, ids_out, squares_out, send, recv, send_sq, recv_sq
):
    seq, ch = lax.axis_index("seq"), lax.axis_index("ch")
    barrier = pltpu.get_barrier_semaphore()
    for d in range(1, seq_count):
        pl.semaphore_signal(
            barrier, inc=1, device_id=(lax.rem(seq + d, seq_count), ch), device_id_type=MESH
        )
    for d in range(1, ch_count):
        pl.semaphore_signal(
            barrier, inc=1, device_id=(seq, lax.rem(ch + d, ch_count)), device_id_type=MESH
        )
    pl.semaphore_wait(barrier, seq_count + ch_count - 2)
    copies = []
    for d in range(1, ch_count):
        copies.append(
            pltpu.make_async_remote_copy(
                src_ref=squares_ref,
                dst_ref=squares_out.at[ch],
                send_sem=send_sq.at[d],
                recv_sem=recv_sq.at[d],
                device_id=(seq, lax.rem(ch + d, ch_count)),
                device_id_type=MESH,
            )
        )
    for d in range(1, seq_count):
        copies.append(
            pltpu.make_async_remote_copy(
                src_ref=ids_ref,
                dst_ref=ids_out.at[seq],
                send_sem=send.at[d],
                recv_sem=recv.at[d],
                device_id=(lax.rem(seq + d, seq_count), ch),
                device_id_type=MESH,
            )
        )
    for copy in copies:
        copy.start()
    ids_out[seq] = ids_ref[...]
    squares_out[ch] = squares_ref[...]
    for copy in copies:
        copy.wait()


def exchange(ids, squares, seq_count, ch_count):
    vmem = pl.BlockSpec(memory_space=pltpu.VMEM)
    dma = pltpu.SemaphoreType.DMA
    return pl.pallas_call(
        functools.partial(exchange_kernel, seq_count, ch_count),
        out_shape=(
            jax.ShapeDtypeStruct((seq_count,) + ids.shape, ids.dtype),
            jax.ShapeDtypeStruct((ch_count,) + squares.shape, squares.dtype),
        ),
        in_specs=[vmem, vmem],
        out_specs=(vmem, vmem),
        scratch_shapes=[dma((seq_count,)), dma((seq_count,)), dma((ch_count,)), dma((ch_count,))],
        compiler_params=pltpu.CompilerParams(collective_id=0, has_side_effects=True),
    )(ids, squares)


def feature_kernel(group, ids_ref, table_ref, taps_ref, first_ref, gated_ref, feats):
    tokens = ids_ref.shape[-1]
    vocab = table_ref.shape[0]
    width = table_ref.shape[1] // 3
    taps = taps_ref.shape[0]

    @pl.when(pl.program_id(0) == 0)
    def _():
        feats[:HISTORY] = jnp.zeros((HISTORY, 3 * width), jnp.float32)

    @pl.when(pl.program_id(0) > 0)
    def _():
        feats[:HISTORY] = feats[tokens:]

    lane = lax.broadcasted_iota(jnp.int32, (LANES, vocab), 1)
    for i in range(tokens // LANES):
        ids = ids_ref[0, :, i * LANES : (i + 1) * LANES].astype(jnp.float32)
        column = jnp.broadcast_to(ids, (LANES, LANES)).T.astype(jnp.int32)[:, :1]
        onehot = (lane == column).astype(jnp.bfloat16)
        feats[HISTORY + i * LANES : HISTORY + (i + 1) * LANES] = jnp.dot(
            onehot, table_ref[...], preferred_element_type=jnp.float32
        )

    def stream(j, start):
        cols = slice(j * width, (j + 1) * width)
        acc = taps_ref[0:1, cols] * feats[start : start + LANES, cols]
        for k in range(1, taps):
            acc = acc + taps_ref[k : k + 1, cols] * feats[start - k : start - k + LANES, cols]
        return acc

    for i in range(tokens // LANES):
        cols = slice(i * LANES, (i + 1) * LANES)
        start = HISTORY + i * LANES
        gated_ref[0, :, cols] = (stream(1, start) * stream(2, start)).T[:group].astype(jnp.bfloat16)
        first_ref[0, :, cols] = stream(0, start).T[:group]


def conv_kernel(
    gated_ref, filter_ref, conv0_ref, skip_ref, t1_ref, t1i_ref, c_ref, s_ref, w2_ref, w2i_ref,
    out_ref, zs, hs, ys, send, send_sem, recv_sem, own_sem,
):
    me, ch = lax.axis_index("seq"), lax.axis_index("ch")
    step_at, steps = pl.program_id(0), pl.num_programs(0)
    blocks, group, tokens = gated_ref.shape
    per = tokens // LANES
    coarse = blocks * per
    f32, bf = jnp.float32, jnp.bfloat16

    @pl.when(step_at == 0)
    def _():
        barrier = pltpu.get_barrier_semaphore()
        for d in range(1, blocks):
            pl.semaphore_signal(
                barrier, inc=1, device_id=(lax.rem(me + d, blocks), ch), device_id_type=MESH
            )
        pl.semaphore_wait(barrier, blocks - 1)

    for s in range(blocks):
        for q in range(per):
            cols = slice(q * LANES, (q + 1) * LANES)
            dst = pl.ds(s * per + q, group, stride=coarse)
            zs[dst, :] = gated_ref[s, :, cols].astype(f32)
            hs[dst, :] = filter_ref[s, :, cols].astype(f32)

    cos, sin = c_ref[...], s_ref[...]

    @pl.loop(0, group // BATCH)
    def _(step):
        base = pl.multiple_of(step * (BATCH * coarse), BATCH * coarse)
        parts = []
        for i in range(BATCH):
            at = pl.ds(base + i * coarse, coarse)
            both = jnp.concatenate([zs[at, :], hs[at, :]], axis=1).astype(bf)
            spread = jnp.dot(t1_ref[...], both, preferred_element_type=f32)
            for side in range(2):
                cols = slice(side * LANES, (side + 1) * LANES)
                re, im = spread[:coarse, cols], spread[coarse:, cols]
                parts.append(
                    jnp.concatenate([re * cos + im * sin, im * cos - re * sin], axis=1).astype(bf)
                )
        spectra = jnp.dot(jnp.concatenate(parts, axis=0), w2_ref[...], preferred_element_type=f32)
        parts = []
        for i in range(BATCH):
            z = spectra[2 * i * coarse : (2 * i + 1) * coarse]
            h = spectra[(2 * i + 1) * coarse : (2 * i + 2) * coarse]
            zr, zi, hr, hi = z[:, :LANES], z[:, LANES:], h[:, :LANES], h[:, LANES:]
            parts.append(jnp.concatenate([zr * hr - zi * hi, zr * hi + zi * hr], axis=1).astype(bf))
        back = jnp.dot(jnp.concatenate(parts, axis=0), w2i_ref[...], preferred_element_type=f32)
        for i in range(0, BATCH, 2):
            cols = []
            for o in range(2):
                p = back[(i + o) * coarse : (i + o + 1) * coarse]
                re, im = p[:, :LANES], p[:, LANES:]
                cols.append(jnp.concatenate([re * cos - im * sin, im * cos + re * sin], axis=0))
            res = jnp.dot(
                t1i_ref[...], jnp.concatenate(cols, axis=1).astype(bf), preferred_element_type=f32
            )
            for o in range(2):
                ys[pl.ds(base + (i + o) * coarse, coarse), :] = res[:, o * LANES : (o + 1) * LANES]

    skip = skip_ref[...]
    for s in range(blocks):
        for q in range(per):
            cols = slice(q * LANES, (q + 1) * LANES)
            conv = ys[pl.ds(s * per + q, group, stride=coarse), :]
            long_out = (conv + skip * gated_ref[s, :, cols].astype(f32)).astype(bf)
            send[step_at, s, :, cols] = (conv0_ref[s, :, cols] * long_out.astype(f32)).astype(bf)

    def rows_of(g):
        return out_ref.at[me, pl.ds(pl.multiple_of(g * group, group), group), :]

    def to_peer(g, d):
        peer = lax.rem(me + d, blocks)
        return pltpu.make_async_remote_copy(
            src_ref=send.at[g, peer],
            dst_ref=rows_of(g),
            send_sem=send_sem.at[g, d],
            recv_sem=recv_sem.at[g, d],
            device_id=(peer, ch),
            device_id_type=MESH,
        )

    def to_self(g):
        return pltpu.make_async_copy(send.at[g, me], rows_of(g), own_sem.at[g])

    @pl.loop(1, blocks)
    def _(d):
        to_peer(step_at, d).start()

    to_self(step_at).start()

    @pl.when(step_at == steps - 1)
    def _():
        @pl.loop(0, steps)
        def _(g):
            to_self(g).wait()

            @pl.loop(1, blocks)
            def _(d):
                to_peer(g, d).wait()


def features(ids, table, taps_rows, group):
    blocks, _, tokens = ids.shape
    vocab, wide = table.shape
    return pl.pallas_call(
        functools.partial(feature_kernel, group),
        grid=(blocks,),
        out_shape=(
            jax.ShapeDtypeStruct((blocks, group, tokens), jnp.float32),
            jax.ShapeDtypeStruct((blocks, group, tokens), jnp.bfloat16),
        ),
        in_specs=[
            pl.BlockSpec((1, 1, tokens), lambda i: (i, 0, 0)),
            pl.BlockSpec(table.shape, lambda i: (0, 0)),
            pl.BlockSpec(taps_rows.shape, lambda i: (0, 0)),
        ],
        out_specs=(
            pl.BlockSpec((1, group, tokens), lambda i: (i, 0, 0)),
            pl.BlockSpec((1, group, tokens), lambda i: (i, 0, 0)),
        ),
        scratch_shapes=[pltpu.VMEM((HISTORY + tokens, wide), jnp.float32)],
        compiler_params=pltpu.CompilerParams(vmem_limit_bytes=VMEM_LIMIT),
        cost_estimate=pl.CostEstimate(
            flops=2 * wide * vocab * blocks * tokens,
            bytes_accessed=blocks * group * tokens * 6,
            transcendentals=0,
        ),
    )(ids, table, taps_rows)


def convolve(gated, filt, conv0, skip_rows):
    blocks, group, tokens = gated.shape
    length = blocks * tokens
    coarse = length // LANES
    tables = transform_tables(length)
    groups = group // GROUP
    dma = pltpu.SemaphoreType.DMA
    whole = lambda t: pl.BlockSpec(t.shape, lambda i: (0, 0))
    rows = pl.BlockSpec((blocks, GROUP, tokens), lambda i: (0, i, 0))
    return pl.pallas_call(
        conv_kernel,
        grid=(groups,),
        out_shape=jax.ShapeDtypeStruct((blocks, group, tokens), jnp.bfloat16),
        in_specs=[rows, rows, rows, pl.BlockSpec((GROUP, 1), lambda i: (i, 0))]
        + [whole(t) for t in tables],
        out_specs=pl.BlockSpec(memory_space=pl.ANY),
        scratch_shapes=[pltpu.VMEM((GROUP * coarse, LANES), jnp.float32)] * 3
        + [
            pltpu.VMEM((groups, blocks, GROUP, tokens), jnp.bfloat16),
            dma((groups, blocks)),
            dma((groups, blocks)),
            dma((groups,)),
        ],
        compiler_params=pltpu.CompilerParams(
            vmem_limit_bytes=VMEM_LIMIT, collective_id=1, has_side_effects=True
        ),
        cost_estimate=pl.CostEstimate(
            flops=2 * group * coarse * 4 * 256 * 256,
            bytes_accessed=blocks * group * tokens * 10,
            transcendentals=0,
        ),
    )(gated, filt, conv0, skip_rows, *tables)


def shards(token_ids, embedding, projected, short_taps, long_filter, skip_gain):
    seq_count = lax.axis_size("seq")
    seq_index = lax.axis_index("seq")
    local_ch, vocab = embedding.shape
    tokens = token_ids.shape[0]
    taps = short_taps.shape[0]
    group = local_ch // seq_count
    start = seq_index * group

    values = embedding.astype(jnp.float32)
    squares = jnp.sum(values * values, axis=0)[None, :]
    ids, squares = exchange(token_ids[None, :], squares, seq_count, lax.axis_size("ch"))
    long_filter, ids = lax.optimization_barrier((long_filter, ids))
    filt = lax.all_to_all(
        long_filter.reshape(seq_count, group, tokens), "seq", split_axis=0, concat_axis=0, tiled=True
    )
    vocab_scale = 1.0 / jnp.sqrt(jnp.sum(squares, axis=0) / MIXER_CHANNELS + EPSILON)
    own = lax.dynamic_slice_in_dim(projected, start, group, axis=1)
    table = (own.astype(jnp.float32) * vocab_scale).astype(jnp.bfloat16)
    taps_rows = lax.dynamic_slice_in_dim(short_taps, start, group, axis=2)
    width = -(-group // LANES) * LANES
    if width != group:
        table = jnp.pad(table, ((0, 0), (0, width - group), (0, 0)))
        taps_rows = jnp.pad(taps_rows, ((0, 0), (0, 0), (0, width - group)))
    conv0, gated = features(
        ids, table.reshape(3 * width, vocab).T, taps_rows.reshape(taps, 3 * width), group
    )
    skip_rows = lax.dynamic_slice_in_dim(skip_gain, start, group)[:, None]
    return convolve(gated, filt, conv0, skip_rows).reshape(local_ch, tokens)


def solution(mesh):
    placed = (
        P("seq"),
        P("ch", None),
        P(None, "ch", None),
        P(None, None, "ch"),
        P("ch", "seq"),
        P("ch"),
    )
    return jax.shard_map(
        shards, mesh=mesh, in_specs=placed, out_specs=P("ch", "seq"), check_vma=False
    )
```

```python
import functools
import math

import jax
import jax.numpy as jnp
import numpy as np
from jax import lax
from jax.experimental import pallas as pl
from jax.experimental.pallas import tpu as pltpu
from jax.sharding import PartitionSpec as P

MIXER_CHANNELS = 4096
EPSILON = 1e-06
LANES = 128
GROUP = 16
BATCH = 8
HISTORY = 8
VMEM_LIMIT = 56 * 1024 * 1024
MESH = pl.DeviceIdType.MESH


def transform_tables(length):
    coarse = length // LANES
    k1 = np.arange(coarse)[:, None] + 0.25
    phi = 2.0 * np.pi * k1 * np.arange(coarse)[None, :] / coarse
    first = np.concatenate([np.cos(phi), -np.sin(phi)], axis=0)
    psi = 2.0 * np.pi * k1 * np.arange(LANES)[None, :] / length
    fine = np.arange(LANES)
    chi = 2.0 * np.pi * (fine[:, None] * fine[None, :] % LANES) / LANES
    c, s = np.cos(chi), np.sin(chi)
    second = np.block([[c, -s], [s, c]])
    second_inv = np.block([[c, s], [-s, c]])
    bf = jnp.bfloat16
    return (
        jnp.asarray(first, bf),
        jnp.asarray(first.T / length, bf),
        jnp.asarray(np.cos(psi), jnp.float32),
        jnp.asarray(np.sin(psi), jnp.float32),
        jnp.asarray(second, bf),
        jnp.asarray(second_inv, bf),
    )


def mixer_kernel(
    seq_count, ch_count,
    ids_ref, squares_ref, proj_ref, taps_ref, filter_ref, skip_ref,
    t1_ref, t1i_ref, c_ref, s_ref, w2_ref, w2i_ref,
    out_ref,
    ids_all, squares_all, table, feats, first, zs, filt, hs, ys, send,
    ids_send, ids_recv, sq_send, sq_recv, filt_send, filt_recv, filt_own, out_send, out_recv, out_own,
):
    me, ch = lax.axis_index("seq"), lax.axis_index("ch")
    step, steps = pl.program_id(0), pl.num_programs(0)
    groups, blocks, rows, tokens = filt.shape
    group = groups * rows
    per = tokens // LANES
    coarse = blocks * per
    vocab = table.shape[0]
    width = table.shape[1] // 3
    taps = taps_ref.shape[0]
    f32, bf = jnp.float32, jnp.bfloat16

    def rows_of(g):
        return pl.ds(pl.multiple_of(g * rows, rows), rows)

    def remote(src, dst, sent, received, device):
        return pltpu.make_async_remote_copy(
            src_ref=src, dst_ref=dst, send_sem=sent, recv_sem=received,
            device_id=device, device_id_type=MESH,
        )

    def along_seq(d):
        return (lax.rem(me + d, seq_count), ch)

    def along_ch(d):
        return (me, lax.rem(ch + d, ch_count))

    def filter_to(g, d):
        peer = along_seq(d)
        return remote(
            filter_ref.at[peer[0], rows_of(g), :], filt.at[g, me],
            filt_send.at[g, d], filt_recv.at[g, d], peer,
        )

    def filter_kept(g):
        return pltpu.make_async_copy(
            filter_ref.at[me, rows_of(g), :], filt.at[g, me], filt_own.at[g]
        )

    def result_to(g, d):
        peer = along_seq(d)
        return remote(
            send.at[g, peer[0]], out_ref.at[me, rows_of(g), :],
            out_send.at[g, d], out_recv.at[g, d], peer,
        )

    def result_kept(g):
        return pltpu.make_async_copy(send.at[g, me], out_ref.at[me, rows_of(g), :], out_own.at[g])

    @pl.when(step == 0)
    def _():
        barrier = pltpu.get_barrier_semaphore()
        for d in range(1, seq_count):
            pl.semaphore_signal(barrier, inc=1, device_id=along_seq(d), device_id_type=MESH)
        for d in range(1, ch_count):
            pl.semaphore_signal(barrier, inc=1, device_id=along_ch(d), device_id_type=MESH)
        pl.semaphore_wait(barrier, seq_count + ch_count - 2)
        small = [
            remote(squares_ref, squares_all.at[ch], sq_send.at[d], sq_recv.at[d], along_ch(d))
            for d in range(1, ch_count)
        ] + [
            remote(ids_ref, ids_all.at[me], ids_send.at[d], ids_recv.at[d], along_seq(d))
            for d in range(1, seq_count)
        ]
        for copy in small:
            copy.start()

        @pl.loop(0, groups)
        def _(g):
            @pl.loop(1, blocks)
            def _(d):
                filter_to(g, d).start()

            filter_kept(g).start()

        ids_all[me] = ids_ref[...]
        squares_all[ch] = squares_ref[...]
        feats[:HISTORY] = jnp.zeros((HISTORY, 3 * width), f32)
        for copy in small:
            copy.wait()
        total = squares_all[0]
        for other in range(1, ch_count):
            total = total + squares_all[other]
        scale = 1.0 / jnp.sqrt(total / MIXER_CHANNELS + EPSILON)
        for v in range(vocab // LANES):
            at = slice(v * LANES, (v + 1) * LANES)
            column = jnp.broadcast_to(scale[:, at], (LANES, LANES)).T[:, :1]
            table[at] = (proj_ref[at].astype(f32) * column).astype(bf)

    @pl.when(step < blocks)
    def _():
        @pl.when(step > 0)
        def _():
            feats[:HISTORY] = feats[tokens:]

        lane = lax.broadcasted_iota(jnp.int32, (LANES, vocab), 1).astype(f32)
        for i in range(per):
            ids = ids_all[step, :, i * LANES : (i + 1) * LANES].astype(f32)
            column = jnp.broadcast_to(ids, (LANES, LANES)).T[:, :1]
            onehot = (lane == column).astype(bf)
            feats[HISTORY + i * LANES : HISTORY + (i + 1) * LANES] = jnp.dot(
                onehot, table[...], preferred_element_type=f32
            )

        def stream(j, start):
            cols = slice(j * width, (j + 1) * width)
            acc = taps_ref[0:1, cols] * feats[start : start + LANES, cols]
            for k in range(1, taps):
                acc = acc + taps_ref[k : k + 1, cols] * feats[start - k : start - k + LANES, cols]
            return acc

        for i in range(per):
            start = HISTORY + i * LANES
            gated = (stream(1, start) * stream(2, start)).astype(bf).astype(f32)
            zs[pl.ds(step * per + i, group, stride=coarse), :] = gated.T[:group]
            first[step, :, i * LANES : (i + 1) * LANES] = stream(0, start).T[:group]

    @pl.when(step >= blocks)
    def _():
        g = step - blocks
        filter_kept(g).wait()

        @pl.loop(1, blocks)
        def _(d):
            filter_to(g, d).wait()

        for s in range(blocks):
            for q in range(per):
                cols = slice(q * LANES, (q + 1) * LANES)
                hs[pl.ds(s * per + q, rows, stride=coarse), :] = filt[g, s, :, cols].astype(f32)

        cos, sin = c_ref[...], s_ref[...]

        @pl.loop(0, rows // BATCH)
        def _(turn):
            base = pl.multiple_of(turn * (BATCH * coarse), BATCH * coarse)
            zbase = pl.multiple_of((g * rows + turn * BATCH) * coarse, BATCH * coarse)
            parts = []
            for i in range(BATCH):
                z = zs[pl.ds(zbase + i * coarse, coarse), :]
                h = hs[pl.ds(base + i * coarse, coarse), :]
                both = jnp.concatenate([z, h], axis=1).astype(bf)
                spread = jnp.dot(t1_ref[...], both, preferred_element_type=f32)
                for side in range(2):
                    cols = slice(side * LANES, (side + 1) * LANES)
                    re, im = spread[:coarse, cols], spread[coarse:, cols]
                    parts.append(
                        jnp.concatenate([re * cos + im * sin, im * cos - re * sin], axis=1).astype(bf)
                    )
            spectra = jnp.dot(
                jnp.concatenate(parts, axis=0), w2_ref[...], preferred_element_type=f32
            )
            parts = []
            for i in range(BATCH):
                z = spectra[2 * i * coarse : (2 * i + 1) * coarse]
                h = spectra[(2 * i + 1) * coarse : (2 * i + 2) * coarse]
                zr, zi, hr, hi = z[:, :LANES], z[:, LANES:], h[:, :LANES], h[:, LANES:]
                parts.append(
                    jnp.concatenate([zr * hr - zi * hi, zr * hi + zi * hr], axis=1).astype(bf)
                )
            back = jnp.dot(jnp.concatenate(parts, axis=0), w2i_ref[...], preferred_element_type=f32)
            for i in range(0, BATCH, 2):
                cols = []
                for o in range(2):
                    p = back[(i + o) * coarse : (i + o + 1) * coarse]
                    re, im = p[:, :LANES], p[:, LANES:]
                    cols.append(jnp.concatenate([re * cos - im * sin, im * cos + re * sin], axis=0))
                res = jnp.dot(
                    t1i_ref[...], jnp.concatenate(cols, axis=1).astype(bf), preferred_element_type=f32
                )
                for o in range(2):
                    skip = skip_ref[g * rows + turn * BATCH + i + o]
                    z = zs[pl.ds(zbase + (i + o) * coarse, coarse), :]
                    ys[pl.ds(base + (i + o) * coarse, coarse), :] = (
                        res[:, o * LANES : (o + 1) * LANES] + skip * z
                    )

        for s in range(blocks):
            for q in range(per):
                cols = slice(q * LANES, (q + 1) * LANES)
                long_out = ys[pl.ds(s * per + q, rows, stride=coarse), :].astype(bf)
                send[g, s, :, cols] = (first[s, rows_of(g), cols] * long_out.astype(f32)).astype(bf)

        @pl.loop(1, blocks)
        def _(d):
            result_to(g, d).start()

        result_kept(g).start()

    @pl.when(step == steps - 1)
    def _():
        @pl.loop(0, groups)
        def _(g):
            result_kept(g).wait()

            @pl.loop(1, blocks)
            def _(d):
                result_to(g, d).wait()


def mix(ids, squares, proj, taps_rows, filt, skip, ch_count):
    blocks, group, tokens = filt.shape
    length = blocks * tokens
    coarse = length // LANES
    groups = group // GROUP
    vocab, wide = proj.shape
    tables = transform_tables(length)
    f32, bf = jnp.float32, jnp.bfloat16
    dma, vmem = pltpu.SemaphoreType.DMA, pltpu.VMEM
    whole = lambda t: pl.BlockSpec(t.shape, lambda i: (0, 0))
    anywhere = pl.BlockSpec(memory_space=pl.ANY)
    return pl.pallas_call(
        functools.partial(mixer_kernel, blocks, ch_count),
        grid=(blocks + groups,),
        out_shape=jax.ShapeDtypeStruct((blocks, group, tokens), bf),
        in_specs=[whole(ids), whole(squares), whole(proj), whole(taps_rows), anywhere]
        + [pl.BlockSpec(memory_space=pltpu.SMEM)]
        + [whole(t) for t in tables],
        out_specs=anywhere,
        scratch_shapes=[
            vmem((blocks, 1, tokens), jnp.int32),
            vmem((ch_count, 1, vocab), f32),
            vmem((vocab, wide), bf),
            vmem((HISTORY + tokens, wide), f32),
            vmem((blocks, group, tokens), f32),
            vmem((group * coarse, LANES), f32),
            vmem((groups, blocks, GROUP, tokens), bf),
            vmem((GROUP * coarse, LANES), f32),
            vmem((GROUP * coarse, LANES), f32),
            vmem((groups, blocks, GROUP, tokens), bf),
            dma((blocks,)),
            dma((blocks,)),
            dma((ch_count,)),
            dma((ch_count,)),
            dma((groups, blocks)),
            dma((groups, blocks)),
            dma((groups,)),
            dma((groups, blocks)),
            dma((groups, blocks)),
            dma((groups,)),
        ],
        compiler_params=pltpu.CompilerParams(
            vmem_limit_bytes=VMEM_LIMIT, collective_id=0, has_side_effects=True
        ),
        cost_estimate=pl.CostEstimate(
            flops=2 * group * coarse * 4 * 256 * 256 + 2 * wide * vocab * length,
            bytes_accessed=group * length * 4,
            transcendentals=0,
        ),
    )(ids, squares, proj, taps_rows, filt, skip, *tables)


def shards(token_ids, embedding, projected, short_taps, long_filter, skip_gain):
    seq_count = lax.axis_size("seq")
    seq_index = lax.axis_index("seq")
    local_ch, vocab = embedding.shape
    tokens = token_ids.shape[0]
    taps = short_taps.shape[0]
    group = local_ch // seq_count
    start = seq_index * group

    values = embedding.astype(jnp.float32)
    squares = jnp.sum(values * values, axis=0)[None, :]
    proj = lax.dynamic_slice_in_dim(projected, start, group, axis=1)
    taps_rows = lax.dynamic_slice_in_dim(short_taps, start, group, axis=2)
    skip = lax.dynamic_slice_in_dim(skip_gain, start, group)
    width = -(-group // LANES) * LANES
    if width != group:
        proj = jnp.pad(proj, ((0, 0), (0, width - group), (0, 0)))
        taps_rows = jnp.pad(taps_rows, ((0, 0), (0, 0), (0, width - group)))
    mixed = mix(
        token_ids[None, :],
        squares,
        proj.reshape(3 * width, vocab).T,
        taps_rows.reshape(taps, 3 * width),
        long_filter.reshape(seq_count, group, tokens),
        skip,
        lax.axis_size("ch"),
    )
    return mixed.reshape(local_ch, tokens)


def solution(mesh):
    placed = (
        P("seq"),
        P("ch", None),
        P(None, "ch", None),
        P(None, None, "ch"),
        P("ch", "seq"),
        P("ch"),
    )
    return jax.shard_map(
        shards, mesh=mesh, in_specs=placed, out_specs=P("ch", "seq"), check_vma=False
    )
```

```python
import functools
import math

import jax
import jax.numpy as jnp
import numpy as np
from jax import lax
from jax.experimental import pallas as pl
from jax.experimental.pallas import tpu as pltpu
from jax.sharding import PartitionSpec as P

MIXER_CHANNELS = 4096
EPSILON = 1e-06
LANES = 128
GROUP = 16
BATCH = 8
HISTORY = 8
VMEM_LIMIT = 56 * 1024 * 1024
MESH = pl.DeviceIdType.MESH


def transform_tables(length):
    coarse = length // LANES
    k1 = np.arange(coarse)[:, None] + 0.25
    phi = 2.0 * np.pi * k1 * np.arange(coarse)[None, :] / coarse
    first = np.concatenate([np.cos(phi), -np.sin(phi)], axis=0)
    psi = 2.0 * np.pi * k1 * np.arange(LANES)[None, :] / length
    fine = np.arange(LANES)
    chi = 2.0 * np.pi * (fine[:, None] * fine[None, :] % LANES) / LANES
    c, s = np.cos(chi), np.sin(chi)
    second = np.block([[c, -s], [s, c]])
    second_inv = np.block([[c, s], [-s, c]])
    bf = jnp.bfloat16
    return (
        jnp.asarray(first, bf),
        jnp.asarray(first.T / length, bf),
        jnp.asarray(np.cos(psi), jnp.float32),
        jnp.asarray(np.sin(psi), jnp.float32),
        jnp.asarray(second, jnp.float32),
        jnp.asarray(second_inv, jnp.float32),
    )


def mixer_kernel(
    seq_count, ch_count, sliced,
    ids_ref, emb_ref, proj_ref, short_ref, filter_ref, skip_ref,
    t1_ref, t1i_ref, c_ref, s_ref, w2_wide, w2i_wide,
    out_ref,
    w2_ref, w2i_ref,
    ids_all, squares_ref, squares_all, proj, taps_ref, table, feats, first, zs, filt, hs, ys, send,
    proj_sem, ids_send, ids_recv, sq_send, sq_recv, filt_send, filt_recv, filt_own, out_send, out_recv, out_own,
):
    me, ch = lax.axis_index("seq"), lax.axis_index("ch")
    step, steps = pl.program_id(0), pl.num_programs(0)
    groups, blocks, rows, tokens = filt.shape
    group = groups * rows
    per = tokens // LANES
    coarse = blocks * per
    vocab = table.shape[0]
    width = table.shape[1] // 3
    taps = taps_ref.shape[0]
    f32, bf = jnp.float32, jnp.bfloat16

    def rows_of(g):
        return pl.ds(pl.multiple_of(g * rows, rows), rows)

    def remote(src, dst, sent, received, device):
        return pltpu.make_async_remote_copy(
            src_ref=src, dst_ref=dst, send_sem=sent, recv_sem=received,
            device_id=device, device_id_type=MESH,
        )

    def along_seq(d):
        return (lax.rem(me + d, seq_count), ch)

    def along_ch(d):
        return (me, lax.rem(ch + d, ch_count))

    def filter_to(g, d):
        peer = along_seq(d)
        return remote(
            filter_ref.at[peer[0], rows_of(g), :], filt.at[g, me],
            filt_send.at[g, d], filt_recv.at[g, d], peer,
        )

    def filter_kept(g):
        return pltpu.make_async_copy(
            filter_ref.at[me, rows_of(g), :], filt.at[g, me], filt_own.at[g]
        )

    def result_to(g, d):
        peer = along_seq(d)
        return remote(
            send.at[g, peer[0]], out_ref.at[me, rows_of(g), :],
            out_send.at[g, d], out_recv.at[g, d], peer,
        )

    def result_kept(g):
        return pltpu.make_async_copy(send.at[g, me], out_ref.at[me, rows_of(g), :], out_own.at[g])

    @pl.when(step == 0)
    def _():
        offset = 0 if sliced else pl.multiple_of(me * group, LANES)
        loads = [
            pltpu.make_async_copy(proj_ref.at[j, pl.ds(offset, width), :], proj.at[j], proj_sem.at[j])
            for j in range(3)
        ]
        for copy in loads:
            copy.start()
        barrier = pltpu.get_barrier_semaphore()
        for d in range(1, seq_count):
            pl.semaphore_signal(barrier, inc=1, device_id=along_seq(d), device_id_type=MESH)
        for d in range(1, ch_count):
            pl.semaphore_signal(barrier, inc=1, device_id=along_ch(d), device_id_type=MESH)
        chunk = LANES

        def add_chunk(i, total):
            values = emb_ref[pl.ds(pl.multiple_of(i * chunk, chunk), chunk), :].astype(f32)
            return total + jnp.sum(values * values, axis=0, keepdims=True)

        squares_ref[...] = lax.fori_loop(
            0, emb_ref.shape[0] // chunk, add_chunk, jnp.zeros((1, vocab), f32)
        )
        pl.semaphore_wait(barrier, seq_count + ch_count - 2)
        small = [
            remote(squares_ref, squares_all.at[ch], sq_send.at[d], sq_recv.at[d], along_ch(d))
            for d in range(1, ch_count)
        ] + [
            remote(ids_ref, ids_all.at[me], ids_send.at[d], ids_recv.at[d], along_seq(d))
            for d in range(1, seq_count)
        ]
        for copy in small:
            copy.start()

        @pl.loop(0, groups)
        def _(g):
            @pl.loop(1, blocks)
            def _(d):
                filter_to(g, d).start()

            filter_kept(g).start()

        ids_all[me] = ids_ref[...]
        squares_all[ch] = squares_ref[...]
        feats[:HISTORY] = jnp.zeros((HISTORY, 3 * width), f32)
        for j in range(3):
            taps_ref[:, j * width : (j + 1) * width] = short_ref[j, :, pl.ds(offset, width)]
        w2_ref[...] = w2_wide[...].astype(bf)
        w2i_ref[...] = w2i_wide[...].astype(bf)
        for copy in loads + small:
            copy.wait()
        total = squares_all[0]
        for other in range(1, ch_count):
            total = total + squares_all[other]
        scale = 1.0 / jnp.sqrt(total / MIXER_CHANNELS + EPSILON)
        for j in range(3):
            for v in range(vocab // LANES):
                at = slice(v * LANES, (v + 1) * LANES)
                scaled = proj[j, :, at].astype(f32) * scale[:, at]
                table[at, j * width : (j + 1) * width] = scaled.T.astype(bf)

    @pl.when(step < blocks)
    def _():
        @pl.when(step > 0)
        def _():
            feats[:HISTORY] = feats[tokens:]

        lane = lax.broadcasted_iota(jnp.int32, (LANES, vocab), 1).astype(f32)
        for i in range(per):
            ids = ids_all[step, :, i * LANES : (i + 1) * LANES].astype(f32)
            column = jnp.broadcast_to(ids, (LANES, LANES)).T
            onehot = (lane == jnp.concatenate([column] * (vocab // LANES), axis=1)).astype(bf)
            feats[HISTORY + i * LANES : HISTORY + (i + 1) * LANES] = jnp.dot(
                onehot, table[...], preferred_element_type=f32
            )

        def stream(j, start):
            cols = slice(j * width, (j + 1) * width)
            acc = taps_ref[0:1, cols] * feats[start : start + LANES, cols]
            for k in range(1, taps):
                acc = acc + taps_ref[k : k + 1, cols] * feats[start - k : start - k + LANES, cols]
            return acc

        for i in range(per):
            start = HISTORY + i * LANES
            gated = (stream(1, start) * stream(2, start)).astype(bf).astype(f32)
            zs[pl.ds(step * per + i, group, stride=coarse), :] = gated.T[:group]
            first[step, :, i * LANES : (i + 1) * LANES] = stream(0, start).T[:group]

    @pl.when(step >= blocks)
    def _():
        g = step - blocks
        filter_kept(g).wait()

        @pl.loop(1, blocks)
        def _(d):
            filter_to(g, d).wait()

        for s in range(blocks):
            for q in range(per):
                cols = slice(q * LANES, (q + 1) * LANES)
                hs[pl.ds(s * per + q, rows, stride=coarse), :] = filt[g, s, :, cols].astype(f32)

        cos, sin = c_ref[...], s_ref[...]

        for turn in range(rows // BATCH):
            base = turn * BATCH * coarse
            zbase = pl.multiple_of((g * rows + turn * BATCH) * coarse, BATCH * coarse)
            parts = []
            for i in range(BATCH):
                z = zs[pl.ds(zbase + i * coarse, coarse), :]
                h = hs[pl.ds(base + i * coarse, coarse), :]
                both = jnp.concatenate([z, h], axis=1).astype(bf)
                spread = jnp.dot(t1_ref[...], both, preferred_element_type=f32)
                for side in range(2):
                    cols = slice(side * LANES, (side + 1) * LANES)
                    re, im = spread[:coarse, cols], spread[coarse:, cols]
                    parts.append(
                        jnp.concatenate([re * cos + im * sin, im * cos - re * sin], axis=1).astype(bf)
                    )
            spectra = jnp.dot(
                jnp.concatenate(parts, axis=0), w2_ref[...], preferred_element_type=f32
            )
            parts = []
            for i in range(BATCH):
                z = spectra[2 * i * coarse : (2 * i + 1) * coarse]
                h = spectra[(2 * i + 1) * coarse : (2 * i + 2) * coarse]
                zr, zi, hr, hi = z[:, :LANES], z[:, LANES:], h[:, :LANES], h[:, LANES:]
                parts.append(
                    jnp.concatenate([zr * hr - zi * hi, zr * hi + zi * hr], axis=1).astype(bf)
                )
            back = jnp.dot(jnp.concatenate(parts, axis=0), w2i_ref[...], preferred_element_type=f32)
            for i in range(0, BATCH, 2):
                cols = []
                for o in range(2):
                    p = back[(i + o) * coarse : (i + o + 1) * coarse]
                    re, im = p[:, :LANES], p[:, LANES:]
                    cols.append(jnp.concatenate([re * cos - im * sin, im * cos + re * sin], axis=0))
                res = jnp.dot(
                    t1i_ref[...], jnp.concatenate(cols, axis=1).astype(bf), preferred_element_type=f32
                )
                for o in range(2):
                    skip = skip_ref[(0 if sliced else me * group) + g * rows + turn * BATCH + i + o]
                    z = zs[pl.ds(zbase + (i + o) * coarse, coarse), :]
                    ys[pl.ds(base + (i + o) * coarse, coarse), :] = (
                        res[:, o * LANES : (o + 1) * LANES] + skip * z
                    )

        for s in range(blocks):
            for q in range(per):
                cols = slice(q * LANES, (q + 1) * LANES)
                long_out = ys[pl.ds(s * per + q, rows, stride=coarse), :].astype(bf)
                send[g, s, :, cols] = (first[s, rows_of(g), cols] * long_out.astype(f32)).astype(bf)

        @pl.loop(1, blocks)
        def _(d):
            result_to(g, d).start()

        result_kept(g).start()

    @pl.when(step == steps - 1)
    def _():
        @pl.loop(0, groups)
        def _(g):
            result_kept(g).wait()

            @pl.loop(1, blocks)
            def _(d):
                result_to(g, d).wait()


def mix(ids, embedding, projected, short_taps, filt, skip, ch_count, sliced):
    blocks, group, tokens = filt.shape
    length = blocks * tokens
    coarse = length // LANES
    groups = group // GROUP
    vocab = embedding.shape[1]
    taps = short_taps.shape[1]
    width = -(-group // LANES) * LANES
    wide = 3 * width
    tables = transform_tables(length)
    f32, bf = jnp.float32, jnp.bfloat16
    dma, vmem = pltpu.SemaphoreType.DMA, pltpu.VMEM
    whole = lambda t: pl.BlockSpec(t.shape, lambda i: (0,) * t.ndim)
    anywhere = pl.BlockSpec(memory_space=pl.ANY)
    return pl.pallas_call(
        functools.partial(mixer_kernel, blocks, ch_count, sliced),
        grid=(blocks + groups,),
        out_shape=jax.ShapeDtypeStruct((blocks, group, tokens), bf),
        in_specs=[whole(ids), whole(embedding), anywhere, whole(short_taps), anywhere]
        + [pl.BlockSpec(memory_space=pltpu.SMEM)]
        + [whole(t) for t in tables],
        out_specs=anywhere,
        scratch_shapes=[
            vmem((2 * LANES, 2 * LANES), bf),
            vmem((2 * LANES, 2 * LANES), bf),
            vmem((blocks, 1, tokens), jnp.int32),
            vmem((1, vocab), f32),
            vmem((ch_count, 1, vocab), f32),
            vmem((3, width, vocab), bf),
            vmem((taps, wide), f32),
            vmem((vocab, wide), bf),
            vmem((HISTORY + tokens, wide), f32),
            vmem((blocks, group, tokens), f32),
            vmem((group * coarse, LANES), f32),
            vmem((groups, blocks, GROUP, tokens), bf),
            vmem((GROUP * coarse, LANES), f32),
            vmem((GROUP * coarse, LANES), f32),
            vmem((groups, blocks, GROUP, tokens), bf),
            dma((3,)),
            dma((blocks,)),
            dma((blocks,)),
            dma((ch_count,)),
            dma((ch_count,)),
            dma((groups, blocks)),
            dma((groups, blocks)),
            dma((groups,)),
            dma((groups, blocks)),
            dma((groups, blocks)),
            dma((groups,)),
        ],
        compiler_params=pltpu.CompilerParams(
            vmem_limit_bytes=VMEM_LIMIT, collective_id=0, has_side_effects=True
        ),
        cost_estimate=pl.CostEstimate(
            flops=2 * group * coarse * 4 * 256 * 256 + 2 * wide * vocab * length,
            bytes_accessed=group * length * 4,
            transcendentals=0,
        ),
    )(ids, embedding, projected, short_taps, filt, skip, *tables)


def shards(token_ids, embedding, projected, short_taps, long_filter, skip_gain):
    seq_count = lax.axis_size("seq")
    local_ch = embedding.shape[0]
    tokens = token_ids.shape[0]
    group = local_ch // seq_count
    sliced = group % LANES != 0
    if sliced:
        start = lax.axis_index("seq") * group
        short = LANES - group % LANES
        projected = lax.dynamic_slice_in_dim(projected, start, group, axis=1)
        short_taps = lax.dynamic_slice_in_dim(short_taps, start, group, axis=2)
        skip_gain = lax.dynamic_slice_in_dim(skip_gain, start, group)
        projected = jnp.pad(projected, ((0, 0), (0, short), (0, 0)))
        short_taps = jnp.pad(short_taps, ((0, 0), (0, 0), (0, short)))
    mixed = mix(
        token_ids[None, :],
        embedding,
        projected,
        jnp.transpose(short_taps, (1, 0, 2)),
        long_filter.reshape(seq_count, group, tokens),
        skip_gain,
        lax.axis_size("ch"),
        sliced,
    )
    return mixed.reshape(local_ch, tokens)


def solution(mesh):
    placed = (
        P("seq"),
        P("ch", None),
        P(None, "ch", None),
        P(None, None, "ch"),
        P("ch", "seq"),
        P("ch"),
    )
    return jax.shard_map(
        shards, mesh=mesh, in_specs=placed, out_specs=P("ch", "seq"), check_vma=False
    )
```

```python
import functools
import math

import jax
import jax.numpy as jnp
import numpy as np
from jax import lax
from jax.experimental import pallas as pl
from jax.experimental.pallas import tpu as pltpu
from jax.sharding import PartitionSpec as P

MIXER_CHANNELS = 4096
EPSILON = 1e-06
LANES = 128
GROUP = 16
BATCH = 8
HISTORY = 8
VMEM_LIMIT = 56 * 1024 * 1024
MESH = pl.DeviceIdType.MESH


def transform_tables(length):
    coarse = length // LANES
    k1 = np.arange(coarse)[:, None] + 0.25
    phi = 2.0 * np.pi * k1 * np.arange(coarse)[None, :] / coarse
    first = np.concatenate([np.cos(phi), -np.sin(phi)], axis=0)
    psi = 2.0 * np.pi * k1 * np.arange(LANES)[None, :] / length
    fine = np.arange(LANES)
    chi = 2.0 * np.pi * (fine[:, None] * fine[None, :] % LANES) / LANES
    c, s = np.cos(chi), np.sin(chi)
    second = np.block([[c, -s], [s, c]])
    second_inv = np.block([[c, s], [-s, c]])
    bf = jnp.bfloat16
    return (
        jnp.asarray(first, bf),
        jnp.asarray(first.T / length, bf),
        jnp.asarray(np.cos(psi), jnp.float32),
        jnp.asarray(np.sin(psi), jnp.float32),
        jnp.asarray(second, jnp.float32),
        jnp.asarray(second_inv, jnp.float32),
    )


def mixer_kernel(
    seq_count, ch_count, sliced,
    ids_ref, emb_ref, proj_ref, short_ref, filter_ref, skip_ref,
    t1_ref, t1i_ref, c_ref, s_ref, w2_wide, w2i_wide,
    out_ref,
    w2_ref, w2i_ref,
    ids_all, squares_ref, squares_all, proj, taps_ref, table, feats, first, zs, filt, hs, ys, send,
    proj_sem, ids_send, ids_recv, sq_send, sq_recv, filt_send, filt_recv, filt_own, out_send, out_recv, out_own,
):
    me, ch = lax.axis_index("seq"), lax.axis_index("ch")
    step, steps = pl.program_id(0), pl.num_programs(0)
    groups, blocks, rows, tokens = filt.shape
    group = groups * rows
    per = tokens // LANES
    coarse = blocks * per
    pitch = coarse + 1
    vocab = table.shape[0]
    width = table.shape[1] // 3
    taps = taps_ref.shape[0]
    f32, bf = jnp.float32, jnp.bfloat16

    def rows_of(g):
        return pl.ds(pl.multiple_of(g * rows, rows), rows)

    def remote(src, dst, sent, received, device):
        return pltpu.make_async_remote_copy(
            src_ref=src, dst_ref=dst, send_sem=sent, recv_sem=received,
            device_id=device, device_id_type=MESH,
        )

    def along_seq(d):
        return (lax.rem(me + d, seq_count), ch)

    def along_ch(d):
        return (me, lax.rem(ch + d, ch_count))

    def filter_to(g, d):
        peer = along_seq(d)
        return remote(
            filter_ref.at[peer[0], rows_of(g), :], filt.at[g, me],
            filt_send.at[g, d], filt_recv.at[g, d], peer,
        )

    def filter_kept(g):
        return pltpu.make_async_copy(
            filter_ref.at[me, rows_of(g), :], filt.at[g, me], filt_own.at[g]
        )

    def result_to(g, d):
        peer = along_seq(d)
        return remote(
            send.at[g, peer[0]], out_ref.at[me, rows_of(g), :],
            out_send.at[g, d], out_recv.at[g, d], peer,
        )

    def result_kept(g):
        return pltpu.make_async_copy(send.at[g, me], out_ref.at[me, rows_of(g), :], out_own.at[g])

    @pl.when(step == 0)
    def _():
        offset = 0 if sliced else pl.multiple_of(me * group, LANES)
        loads = [
            pltpu.make_async_copy(proj_ref.at[j, pl.ds(offset, width), :], proj.at[j], proj_sem.at[j])
            for j in range(3)
        ]
        for copy in loads:
            copy.start()
        barrier = pltpu.get_barrier_semaphore()
        for d in range(1, seq_count):
            pl.semaphore_signal(barrier, inc=1, device_id=along_seq(d), device_id_type=MESH)
        for d in range(1, ch_count):
            pl.semaphore_signal(barrier, inc=1, device_id=along_ch(d), device_id_type=MESH)
        chunk = LANES

        def add_chunk(i, total):
            values = emb_ref[pl.ds(pl.multiple_of(i * chunk, chunk), chunk), :].astype(f32)
            return total + jnp.sum(values * values, axis=0, keepdims=True)

        squares_ref[...] = lax.fori_loop(
            0, emb_ref.shape[0] // chunk, add_chunk, jnp.zeros((1, vocab), f32)
        )
        pl.semaphore_wait(barrier, seq_count + ch_count - 2)
        small = [
            remote(squares_ref, squares_all.at[ch], sq_send.at[d], sq_recv.at[d], along_ch(d))
            for d in range(1, ch_count)
        ] + [
            remote(ids_ref, ids_all.at[me], ids_send.at[d], ids_recv.at[d], along_seq(d))
            for d in range(1, seq_count)
        ]
        for copy in small:
            copy.start()

        @pl.loop(0, groups)
        def _(g):
            @pl.loop(1, blocks)
            def _(d):
                filter_to(g, d).start()

            filter_kept(g).start()

        ids_all[me] = ids_ref[...]
        squares_all[ch] = squares_ref[...]
        feats[:HISTORY] = jnp.zeros((HISTORY, 3 * width), f32)
        for j in range(3):
            taps_ref[:, j * width : (j + 1) * width] = short_ref[j, :, pl.ds(offset, width)]
        w2_ref[...] = w2_wide[...].astype(bf)
        w2i_ref[...] = w2i_wide[...].astype(bf)
        for copy in loads + small:
            copy.wait()
        total = squares_all[0]
        for other in range(1, ch_count):
            total = total + squares_all[other]
        scale = 1.0 / jnp.sqrt(total / MIXER_CHANNELS + EPSILON)
        for j in range(3):
            for v in range(vocab // LANES):
                at = slice(v * LANES, (v + 1) * LANES)
                scaled = proj[j, :, at].astype(f32) * scale[:, at]
                table[at, j * width : (j + 1) * width] = scaled.T.astype(bf)

    @pl.when(step < blocks)
    def _():
        @pl.when(step > 0)
        def _():
            feats[:HISTORY] = feats[tokens:]

        lane = lax.broadcasted_iota(jnp.int32, (LANES, vocab), 1).astype(f32)
        for i in range(per):
            ids = ids_all[step, :, i * LANES : (i + 1) * LANES].astype(f32)
            column = jnp.broadcast_to(ids, (LANES, LANES)).T
            onehot = (lane == jnp.concatenate([column] * (vocab // LANES), axis=1)).astype(bf)
            feats[HISTORY + i * LANES : HISTORY + (i + 1) * LANES] = jnp.dot(
                onehot, table[...], preferred_element_type=f32
            )

        def stream(j, start):
            cols = slice(j * width, (j + 1) * width)
            acc = taps_ref[0:1, cols] * feats[start : start + LANES, cols]
            for k in range(1, taps):
                acc = acc + taps_ref[k : k + 1, cols] * feats[start - k : start - k + LANES, cols]
            return acc

        for i in range(per):
            start = HISTORY + i * LANES
            gated = (stream(1, start) * stream(2, start)).astype(bf).astype(f32)
            zs[pl.ds(step * per + i, group, stride=coarse), :] = gated.T[:group]
            first[step, :, i * LANES : (i + 1) * LANES] = stream(0, start).T[:group]

    @pl.when(step >= blocks)
    def _():
        g = step - blocks
        filter_kept(g).wait()

        @pl.loop(1, blocks)
        def _(d):
            filter_to(g, d).wait()

        for s in range(blocks):
            for q in range(per):
                cols = slice(q * LANES, (q + 1) * LANES)
                hs[pl.ds(s * per + q, rows, stride=pitch), :] = filt[g, s, :, cols].astype(f32)

        cos, sin = c_ref[...], s_ref[...]

        for turn in range(rows // BATCH):
            base = turn * BATCH * pitch
            zbase = pl.multiple_of((g * rows + turn * BATCH) * coarse, BATCH * coarse)
            parts = []
            for i in range(BATCH):
                z = zs[pl.ds(zbase + i * coarse, coarse), :]
                h = hs[base + i * pitch : base + i * pitch + coarse, :]
                both = jnp.concatenate([z, h], axis=1).astype(bf)
                spread = jnp.dot(t1_ref[...], both, preferred_element_type=f32)
                for side in range(2):
                    cols = slice(side * LANES, (side + 1) * LANES)
                    re, im = spread[:coarse, cols], spread[coarse:, cols]
                    parts.append(
                        jnp.concatenate([re * cos + im * sin, im * cos - re * sin], axis=1).astype(bf)
                    )
            spectra = jnp.dot(
                jnp.concatenate(parts, axis=0), w2_ref[...], preferred_element_type=f32
            )
            parts = []
            for i in range(BATCH):
                z = spectra[2 * i * coarse : (2 * i + 1) * coarse]
                h = spectra[(2 * i + 1) * coarse : (2 * i + 2) * coarse]
                zr, zi, hr, hi = z[:, :LANES], z[:, LANES:], h[:, :LANES], h[:, LANES:]
                parts.append(
                    jnp.concatenate([zr * hr - zi * hi, zr * hi + zi * hr], axis=1).astype(bf)
                )
            back = jnp.dot(jnp.concatenate(parts, axis=0), w2i_ref[...], preferred_element_type=f32)
            for i in range(0, BATCH, 2):
                cols = []
                for o in range(2):
                    p = back[(i + o) * coarse : (i + o + 1) * coarse]
                    re, im = p[:, :LANES], p[:, LANES:]
                    cols.append(jnp.concatenate([re * cos - im * sin, im * cos + re * sin], axis=0))
                res = jnp.dot(
                    t1i_ref[...], jnp.concatenate(cols, axis=1).astype(bf), preferred_element_type=f32
                )
                for o in range(2):
                    skip = skip_ref[(0 if sliced else me * group) + g * rows + turn * BATCH + i + o]
                    z = zs[pl.ds(zbase + (i + o) * coarse, coarse), :]
                    ys[base + (i + o) * pitch : base + (i + o) * pitch + coarse, :] = (
                        res[:, o * LANES : (o + 1) * LANES] + skip * z
                    )

        for s in range(blocks):
            for q in range(per):
                cols = slice(q * LANES, (q + 1) * LANES)
                long_out = ys[pl.ds(s * per + q, rows, stride=pitch), :].astype(bf)
                send[g, s, :, cols] = (first[s, rows_of(g), cols] * long_out.astype(f32)).astype(bf)

        @pl.loop(1, blocks)
        def _(d):
            result_to(g, d).start()

        result_kept(g).start()

    @pl.when(step == steps - 1)
    def _():
        @pl.loop(0, groups)
        def _(g):
            result_kept(g).wait()

            @pl.loop(1, blocks)
            def _(d):
                result_to(g, d).wait()


def mix(ids, embedding, projected, short_taps, filt, skip, ch_count, sliced):
    blocks, group, tokens = filt.shape
    length = blocks * tokens
    coarse = length // LANES
    groups = group // GROUP
    vocab = embedding.shape[1]
    taps = short_taps.shape[1]
    width = -(-group // LANES) * LANES
    wide = 3 * width
    tables = transform_tables(length)
    f32, bf = jnp.float32, jnp.bfloat16
    dma, vmem = pltpu.SemaphoreType.DMA, pltpu.VMEM
    whole = lambda t: pl.BlockSpec(t.shape, lambda i: (0,) * t.ndim)
    anywhere = pl.BlockSpec(memory_space=pl.ANY)
    return pl.pallas_call(
        functools.partial(mixer_kernel, blocks, ch_count, sliced),
        grid=(blocks + groups,),
        out_shape=jax.ShapeDtypeStruct((blocks, group, tokens), bf),
        in_specs=[whole(ids), whole(embedding), anywhere, whole(short_taps), anywhere]
        + [pl.BlockSpec(memory_space=pltpu.SMEM)]
        + [whole(t) for t in tables],
        out_specs=anywhere,
        scratch_shapes=[
            vmem((2 * LANES, 2 * LANES), bf),
            vmem((2 * LANES, 2 * LANES), bf),
            vmem((blocks, 1, tokens), jnp.int32),
            vmem((1, vocab), f32),
            vmem((ch_count, 1, vocab), f32),
            vmem((3, width, vocab), bf),
            vmem((taps, wide), f32),
            vmem((vocab, wide), bf),
            vmem((HISTORY + tokens, wide), f32),
            vmem((blocks, group, tokens), f32),
            vmem((group * coarse, LANES), f32),
            vmem((groups, blocks, GROUP, tokens), bf),
            vmem((GROUP * (coarse + 1), LANES), f32),
            vmem((GROUP * (coarse + 1), LANES), f32),
            vmem((groups, blocks, GROUP, tokens), bf),
            dma((3,)),
            dma((blocks,)),
            dma((blocks,)),
            dma((ch_count,)),
            dma((ch_count,)),
            dma((groups, blocks)),
            dma((groups, blocks)),
            dma((groups,)),
            dma((groups, blocks)),
            dma((groups, blocks)),
            dma((groups,)),
        ],
        compiler_params=pltpu.CompilerParams(
            vmem_limit_bytes=VMEM_LIMIT, collective_id=0, has_side_effects=True
        ),
        cost_estimate=pl.CostEstimate(
            flops=2 * group * coarse * 4 * 256 * 256 + 2 * wide * vocab * length,
            bytes_accessed=group * length * 4,
            transcendentals=0,
        ),
    )(ids, embedding, projected, short_taps, filt, skip, *tables)


def shards(token_ids, embedding, projected, short_taps, long_filter, skip_gain):
    seq_count = lax.axis_size("seq")
    local_ch = embedding.shape[0]
    tokens = token_ids.shape[0]
    group = local_ch // seq_count
    sliced = group % LANES != 0
    if sliced:
        start = lax.axis_index("seq") * group
        short = LANES - group % LANES
        projected = lax.dynamic_slice_in_dim(projected, start, group, axis=1)
        short_taps = lax.dynamic_slice_in_dim(short_taps, start, group, axis=2)
        skip_gain = lax.dynamic_slice_in_dim(skip_gain, start, group)
        projected = jnp.pad(projected, ((0, 0), (0, short), (0, 0)))
        short_taps = jnp.pad(short_taps, ((0, 0), (0, 0), (0, short)))
    mixed = mix(
        token_ids[None, :],
        embedding,
        projected,
        jnp.transpose(short_taps, (1, 0, 2)),
        long_filter.reshape(seq_count, group, tokens),
        skip_gain,
        lax.axis_size("ch"),
        sliced,
    )
    return mixed.reshape(local_ch, tokens)


def solution(mesh):
    placed = (
        P("seq"),
        P("ch", None),
        P(None, "ch", None),
        P(None, None, "ch"),
        P("ch", "seq"),
        P("ch"),
    )
    return jax.shard_map(
        shards, mesh=mesh, in_specs=placed, out_specs=P("ch", "seq"), check_vma=False
    )
```

```python
import functools
import math

import jax
import jax.numpy as jnp
import numpy as np
from jax import lax
from jax.experimental import pallas as pl
from jax.experimental.pallas import tpu as pltpu
from jax.sharding import PartitionSpec as P

MIXER_CHANNELS = 4096
EPSILON = 1e-06
LANES = 128
GROUP = 16
BATCH = 4
HISTORY = 8
VMEM_LIMIT = 56 * 1024 * 1024
MESH = pl.DeviceIdType.MESH


def transform_tables(length):
    coarse = length // LANES
    k1 = np.arange(coarse)[:, None] + 0.25
    phi = 2.0 * np.pi * k1 * np.arange(coarse)[None, :] / coarse
    first = np.concatenate([np.cos(phi), -np.sin(phi)], axis=0)
    psi = 2.0 * np.pi * k1 * np.arange(LANES)[None, :] / length
    fine = np.arange(LANES)
    chi = 2.0 * np.pi * (fine[:, None] * fine[None, :] % LANES) / LANES
    c, s = np.cos(chi), np.sin(chi)
    second = np.block([[c, -s], [s, c]])
    second_inv = np.block([[c, s], [-s, c]])
    bf = jnp.bfloat16
    return (
        jnp.asarray(first, bf),
        jnp.asarray(first.T / length, bf),
        jnp.asarray(np.cos(psi), jnp.float32),
        jnp.asarray(np.sin(psi), jnp.float32),
        jnp.asarray(second, jnp.float32),
        jnp.asarray(second_inv, jnp.float32),
    )


def mixer_kernel(
    seq_count, ch_count, sliced,
    ids_ref, emb_ref, proj_ref, short_ref, filter_ref, skip_ref,
    t1_ref, t1i_ref, c_ref, s_ref, w2_wide, w2i_wide,
    out_ref,
    w2_ref, w2i_ref,
    ids_all, squares_ref, squares_all, proj, taps_ref, table, feats, first, zs, filt, hs, ys, send,
    proj_sem, ids_send, ids_recv, sq_send, sq_recv, filt_send, filt_recv, filt_own, out_send, out_recv, out_own,
):
    me, ch = lax.axis_index("seq"), lax.axis_index("ch")
    step, steps = pl.program_id(0), pl.num_programs(0)
    groups, blocks, rows, tokens = filt.shape
    group = groups * rows
    per = tokens // LANES
    coarse = blocks * per
    pitch = coarse + 1
    vocab = table.shape[0]
    width = table.shape[1] // 3
    taps = taps_ref.shape[0]
    f32, bf = jnp.float32, jnp.bfloat16

    def rows_of(g):
        return pl.ds(pl.multiple_of(g * rows, rows), rows)

    def remote(src, dst, sent, received, device):
        return pltpu.make_async_remote_copy(
            src_ref=src, dst_ref=dst, send_sem=sent, recv_sem=received,
            device_id=device, device_id_type=MESH,
        )

    def along_seq(d):
        return (lax.rem(me + d, seq_count), ch)

    def along_ch(d):
        return (me, lax.rem(ch + d, ch_count))

    def filter_to(g, d):
        peer = along_seq(d)
        return remote(
            filter_ref.at[peer[0], rows_of(g), :], filt.at[g, me],
            filt_send.at[g, d], filt_recv.at[g, d], peer,
        )

    def filter_kept(g):
        return pltpu.make_async_copy(
            filter_ref.at[me, rows_of(g), :], filt.at[g, me], filt_own.at[g]
        )

    def result_to(g, d):
        peer = along_seq(d)
        return remote(
            send.at[g, peer[0]], out_ref.at[me, rows_of(g), :],
            out_send.at[g, d], out_recv.at[g, d], peer,
        )

    def result_kept(g):
        return pltpu.make_async_copy(send.at[g, me], out_ref.at[me, rows_of(g), :], out_own.at[g])

    @pl.when(step == 0)
    def _():
        offset = 0 if sliced else pl.multiple_of(me * group, LANES)
        loads = [
            pltpu.make_async_copy(proj_ref.at[j, pl.ds(offset, width), :], proj.at[j], proj_sem.at[j])
            for j in range(3)
        ]
        for copy in loads:
            copy.start()
        barrier = pltpu.get_barrier_semaphore()
        for d in range(1, seq_count):
            pl.semaphore_signal(barrier, inc=1, device_id=along_seq(d), device_id_type=MESH)
        for d in range(1, ch_count):
            pl.semaphore_signal(barrier, inc=1, device_id=along_ch(d), device_id_type=MESH)
        chunk = LANES

        def add_chunk(i, total):
            values = emb_ref[pl.ds(pl.multiple_of(i * chunk, chunk), chunk), :].astype(f32)
            return total + jnp.sum(values * values, axis=0, keepdims=True)

        squares_ref[...] = lax.fori_loop(
            0, emb_ref.shape[0] // chunk, add_chunk, jnp.zeros((1, vocab), f32)
        )
        pl.semaphore_wait(barrier, seq_count + ch_count - 2)
        small = [
            remote(squares_ref, squares_all.at[ch], sq_send.at[d], sq_recv.at[d], along_ch(d))
            for d in range(1, ch_count)
        ] + [
            remote(ids_ref, ids_all.at[me], ids_send.at[d], ids_recv.at[d], along_seq(d))
            for d in range(1, seq_count)
        ]
        for copy in small:
            copy.start()

        @pl.loop(0, groups)
        def _(g):
            @pl.loop(1, blocks)
            def _(d):
                filter_to(g, d).start()

            filter_kept(g).start()

        ids_all[me] = ids_ref[...]
        squares_all[ch] = squares_ref[...]
        feats[:HISTORY] = jnp.zeros((HISTORY, 3 * width), f32)
        for j in range(3):
            taps_ref[:, j * width : (j + 1) * width] = short_ref[j, :, pl.ds(offset, width)]
        w2_ref[...] = w2_wide[...].astype(bf)
        w2i_ref[...] = w2i_wide[...].astype(bf)
        for copy in loads + small:
            copy.wait()
        total = squares_all[0]
        for other in range(1, ch_count):
            total = total + squares_all[other]
        scale = 1.0 / jnp.sqrt(total / MIXER_CHANNELS + EPSILON)
        for j in range(3):
            for v in range(vocab // LANES):
                at = slice(v * LANES, (v + 1) * LANES)
                scaled = proj[j, :, at].astype(f32) * scale[:, at]
                table[at, j * width : (j + 1) * width] = scaled.T.astype(bf)

    @pl.when(step < blocks)
    def _():
        @pl.when(step > 0)
        def _():
            feats[:HISTORY] = feats[tokens:]

        lane = lax.broadcasted_iota(jnp.int32, (LANES, vocab), 1).astype(f32)
        for i in range(per):
            ids = ids_all[step, :, i * LANES : (i + 1) * LANES].astype(f32)
            column = jnp.broadcast_to(ids, (LANES, LANES)).T
            onehot = (lane == jnp.concatenate([column] * (vocab // LANES), axis=1)).astype(bf)
            feats[HISTORY + i * LANES : HISTORY + (i + 1) * LANES] = jnp.dot(
                onehot, table[...], preferred_element_type=f32
            )

        def stream(j, start):
            cols = slice(j * width, (j + 1) * width)
            acc = taps_ref[0:1, cols] * feats[start : start + LANES, cols]
            for k in range(1, taps):
                acc = acc + taps_ref[k : k + 1, cols] * feats[start - k : start - k + LANES, cols]
            return acc

        for i in range(per):
            start = HISTORY + i * LANES
            gated = (stream(1, start) * stream(2, start)).astype(bf).astype(f32)
            zs[pl.ds(step * per + i, group, stride=coarse), :] = gated.T[:group]
            first[step, :, i * LANES : (i + 1) * LANES] = stream(0, start).T[:group]

    @pl.when(step >= blocks)
    def _():
        g = step - blocks
        filter_kept(g).wait()

        @pl.loop(1, blocks)
        def _(d):
            filter_to(g, d).wait()

        for s in range(blocks):
            for q in range(per):
                cols = slice(q * LANES, (q + 1) * LANES)
                hs[pl.ds(s * per + q, rows, stride=pitch), :] = filt[g, s, :, cols].astype(f32)

        cos, sin = c_ref[...], s_ref[...]

        for turn in range(rows // BATCH):
            base = turn * BATCH * pitch
            zbase = pl.multiple_of((g * rows + turn * BATCH) * coarse, BATCH * coarse)
            parts = []
            for i in range(BATCH):
                z = zs[pl.ds(zbase + i * coarse, coarse), :]
                h = hs[base + i * pitch : base + i * pitch + coarse, :]
                both = jnp.concatenate([z, h], axis=1).astype(bf)
                spread = jnp.dot(t1_ref[...], both, preferred_element_type=f32)
                for side in range(2):
                    cols = slice(side * LANES, (side + 1) * LANES)
                    re, im = spread[:coarse, cols], spread[coarse:, cols]
                    parts.append(
                        jnp.concatenate([re * cos + im * sin, im * cos - re * sin], axis=1).astype(bf)
                    )
            spectra = jnp.dot(
                jnp.concatenate(parts, axis=0), w2_ref[...], preferred_element_type=f32
            )
            parts = []
            for i in range(BATCH):
                z = spectra[2 * i * coarse : (2 * i + 1) * coarse]
                h = spectra[(2 * i + 1) * coarse : (2 * i + 2) * coarse]
                zr, zi, hr, hi = z[:, :LANES], z[:, LANES:], h[:, :LANES], h[:, LANES:]
                parts.append(
                    jnp.concatenate([zr * hr - zi * hi, zr * hi + zi * hr], axis=1).astype(bf)
                )
            back = jnp.dot(jnp.concatenate(parts, axis=0), w2i_ref[...], preferred_element_type=f32)
            for i in range(0, BATCH, 2):
                cols = []
                for o in range(2):
                    p = back[(i + o) * coarse : (i + o + 1) * coarse]
                    re, im = p[:, :LANES], p[:, LANES:]
                    cols.append(jnp.concatenate([re * cos - im * sin, im * cos + re * sin], axis=0))
                res = jnp.dot(
                    t1i_ref[...], jnp.concatenate(cols, axis=1).astype(bf), preferred_element_type=f32
                )
                for o in range(2):
                    skip = skip_ref[(0 if sliced else me * group) + g * rows + turn * BATCH + i + o]
                    z = zs[pl.ds(zbase + (i + o) * coarse, coarse), :]
                    ys[base + (i + o) * pitch : base + (i + o) * pitch + coarse, :] = (
                        res[:, o * LANES : (o + 1) * LANES] + skip * z
                    )

        for s in range(blocks):
            for q in range(per):
                cols = slice(q * LANES, (q + 1) * LANES)
                long_out = ys[pl.ds(s * per + q, rows, stride=pitch), :].astype(bf)
                send[g, s, :, cols] = (first[s, rows_of(g), cols] * long_out.astype(f32)).astype(bf)

        @pl.loop(1, blocks)
        def _(d):
            result_to(g, d).start()

        result_kept(g).start()

    @pl.when(step == steps - 1)
    def _():
        @pl.loop(0, groups)
        def _(g):
            result_kept(g).wait()

            @pl.loop(1, blocks)
            def _(d):
                result_to(g, d).wait()


def mix(ids, embedding, projected, short_taps, filt, skip, ch_count, sliced):
    blocks, group, tokens = filt.shape
    length = blocks * tokens
    coarse = length // LANES
    groups = group // GROUP
    vocab = embedding.shape[1]
    taps = short_taps.shape[1]
    width = -(-group // LANES) * LANES
    wide = 3 * width
    tables = transform_tables(length)
    f32, bf = jnp.float32, jnp.bfloat16
    dma, vmem = pltpu.SemaphoreType.DMA, pltpu.VMEM
    whole = lambda t: pl.BlockSpec(t.shape, lambda i: (0,) * t.ndim)
    anywhere = pl.BlockSpec(memory_space=pl.ANY)
    return pl.pallas_call(
        functools.partial(mixer_kernel, blocks, ch_count, sliced),
        grid=(blocks + groups,),
        out_shape=jax.ShapeDtypeStruct((blocks, group, tokens), bf),
        in_specs=[whole(ids), whole(embedding), anywhere, whole(short_taps), anywhere]
        + [pl.BlockSpec(memory_space=pltpu.SMEM)]
        + [whole(t) for t in tables],
        out_specs=anywhere,
        scratch_shapes=[
            vmem((2 * LANES, 2 * LANES), bf),
            vmem((2 * LANES, 2 * LANES), bf),
            vmem((blocks, 1, tokens), jnp.int32),
            vmem((1, vocab), f32),
            vmem((ch_count, 1, vocab), f32),
            vmem((3, width, vocab), bf),
            vmem((taps, wide), f32),
            vmem((vocab, wide), bf),
            vmem((HISTORY + tokens, wide), f32),
            vmem((blocks, group, tokens), f32),
            vmem((group * coarse, LANES), f32),
            vmem((groups, blocks, GROUP, tokens), bf),
            vmem((GROUP * (coarse + 1), LANES), f32),
            vmem((GROUP * (coarse + 1), LANES), f32),
            vmem((groups, blocks, GROUP, tokens), bf),
            dma((3,)),
            dma((blocks,)),
            dma((blocks,)),
            dma((ch_count,)),
            dma((ch_count,)),
            dma((groups, blocks)),
            dma((groups, blocks)),
            dma((groups,)),
            dma((groups, blocks)),
            dma((groups, blocks)),
            dma((groups,)),
        ],
        compiler_params=pltpu.CompilerParams(
            vmem_limit_bytes=VMEM_LIMIT, collective_id=0, has_side_effects=True
        ),
        cost_estimate=pl.CostEstimate(
            flops=2 * group * coarse * 4 * 256 * 256 + 2 * wide * vocab * length,
            bytes_accessed=group * length * 4,
            transcendentals=0,
        ),
    )(ids, embedding, projected, short_taps, filt, skip, *tables)


def shards(token_ids, embedding, projected, short_taps, long_filter, skip_gain):
    seq_count = lax.axis_size("seq")
    local_ch = embedding.shape[0]
    tokens = token_ids.shape[0]
    group = local_ch // seq_count
    sliced = group % LANES != 0
    if sliced:
        start = lax.axis_index("seq") * group
        short = LANES - group % LANES
        projected = lax.dynamic_slice_in_dim(projected, start, group, axis=1)
        short_taps = lax.dynamic_slice_in_dim(short_taps, start, group, axis=2)
        skip_gain = lax.dynamic_slice_in_dim(skip_gain, start, group)
        projected = jnp.pad(projected, ((0, 0), (0, short), (0, 0)))
        short_taps = jnp.pad(short_taps, ((0, 0), (0, 0), (0, short)))
    mixed = mix(
        token_ids[None, :],
        embedding,
        projected,
        jnp.transpose(short_taps, (1, 0, 2)),
        long_filter.reshape(seq_count, group, tokens),
        skip_gain,
        lax.axis_size("ch"),
        sliced,
    )
    return mixed.reshape(local_ch, tokens)


def solution(mesh):
    placed = (
        P("seq"),
        P("ch", None),
        P(None, "ch", None),
        P(None, None, "ch"),
        P("ch", "seq"),
        P("ch"),
    )
    return jax.shard_map(
        shards, mesh=mesh, in_specs=placed, out_specs=P("ch", "seq"), check_vma=False
    )
```
